256 devices in a mesh: sta: 4 (over x), ev: 64 (over z, y, core).
Axes of the slice: x: 4, y: 4, z: 8, core: 2. Of those that a mesh axis runs over, the one named last changes fastest.
Arguments:
- traces: bfloat16 [192, 524288], P('sta', 'ev'), parts along dimension 0, may hold values from -55 to 55
- held_count: int32 [256], P('sta'), parts along dimension 0, may hold values from 2 to 62, as said below
- window_owner_table: int32 [256, 62], P('sta'), parts along dimension 0, may hold values from 0 to 2047, as said below
- pick_offset: int32 [256, 62], P(('sta', 'ev')), parts along dimension 0, may hold values from 0 to 8191
- neighbours: int32 [8192, 128], P(('sta', 'ev')), parts along dimension 0, may hold values from 0 to 287, as said below
Outputs:
- correlation: float32 [8192, 61, 128], P(('sta', 'ev')), parts along dimension 0
The draws below stay inside these ranges and needn't reach their ends.
There are 4 independent parts, one for each index of `sta`. The reference program is written for one: setup_inputs(seed, part) draws one part's arguments, and reference() takes and returns one part's arrays. A program takes and returns all parts, laid end to end along the dimension named above; each array names one. Nothing has to cross between parts.
Inputs may be any that keep to these rules, and one draw needn't show every extreme that they name: `held_count`: each count is even and the counts sum to 2048; some holder holds exactly 62. `window_owner_table`: the first held_count[d] entries of row d name the events of holder d's windows; over all holders they name every event slot exactly once; entries 2i and 2i+1 of a row name positions 2j and 2j+1 of one owner; no holder names more than 2 events of one owner, and some holder names exactly that many. Other entries are not read. `pick_offset`: only the first held_count[d] entries of row d are read. `neighbours`: an event of block o names blocks o - q with q <= min(o, 8); its first neighbour lies in block o - min(o, 8).
All inputs are finite; a program needn't handle non-finite values.
Results may differ from the reference program's by a relative error of at most 0.0003.
Values may be sent and summed in bfloat16 or wider, within the bound.
No kernel may reach another device: no remote copies, remote signals or barrier semaphores. Data moves between devices by JAX's collectives and lax.ppermute only.
A program may use at most 128 MiB of HBM per device.

```python
import jax
import jax.numpy as jnp
from jax import lax

COMP = 48
WIN = 256
MAXLAG = 30
K = 128
E_DEV = 32
SEG = 8192
BAND = 8
HCAP = 62
EVENTS = 2048
SAMPLES = 524288
N_EV = 64


def holder_layout(key):
    key = jax.random.fold_in(key, 101)
    first_key, second_key, third_key, fourth_key = jax.random.split(key, 4)
    half_runs = E_DEV // 2
    pair_count = N_EV // 2
    excess = jax.random.randint(first_key, (pair_count,), 0, half_runs)
    excess = excess.at[0].set(half_runs - 1)
    run_counts = jnp.concatenate([half_runs + excess, half_runs - excess])
    run_counts = run_counts[jax.random.permutation(second_key, N_EV)]
    first_run = jnp.cumsum(run_counts) - run_counts
    slot_index = jnp.arange(HCAP, dtype=jnp.int32)
    run_index = first_run[:, None] + slot_index[None, :] // 2
    owner_order = jax.random.permutation(third_key, N_EV)
    owner_device = owner_order[run_index % N_EV]
    table = owner_device * E_DEV + 2 * (run_index // N_EV) + slot_index[None, :] % 2
    is_live = slot_index[None, :] < 2 * run_counts[:, None]
    filler = jax.random.randint(fourth_key, (N_EV, HCAP), 0, EVENTS)
    return ((2 * run_counts).astype(jnp.int32), jnp.where(is_live, table, filler).astype(jnp.int32))


def draw_held_count(key, part):
    return holder_layout(key)[0]


def draw_window_owner_table(key, part):
    return holder_layout(key)[1]


def draw_neighbours(key, part):
    key = jax.random.fold_in(key, 23)
    first_key, second_key = jax.random.split(key)
    row_index = jnp.arange(EVENTS, dtype=jnp.int32)
    reach_most = jnp.minimum(row_index // E_DEV, BAND)
    depth = jax.random.randint(first_key, (EVENTS, K), 0, reach_most[:, None] + 1)
    within = jax.random.randint(second_key, (EVENTS, K), 0, E_DEV)
    depth = depth.at[:, 0].set(reach_most)
    within = within.at[:, 0].set(E_DEV - 1 - row_index % E_DEV)
    return (depth * E_DEV + within).astype(jnp.int32)


def draw_traces(key, part):
    key = jax.random.fold_in(key, 11)
    first_key, second_key, third_key = jax.random.split(key, 3)
    base = jnp.clip(jax.random.normal(first_key, (COMP, SAMPLES), jnp.float32), -6.0, 6.0)
    spread = jnp.exp(jax.random.uniform(second_key, (COMP, 1), jnp.float32, -1.2, 1.2))
    envelope = jnp.exp(jax.random.uniform(third_key, (1, SAMPLES // 64), jnp.float32, -1.0, 1.0))
    return (base * spread * jnp.repeat(envelope, 64, axis=1)).astype(jnp.bfloat16)


def with_ends(result, key, low, top_value):
    extent = result.shape
    place = [jax.random.randint(jax.random.fold_in(key, axis), (), 0, extent[axis]) for axis in range(len(extent))]
    result = result.at[tuple(place)].set(low)
    longest = extent.index(max(extent))
    place[longest] = (place[longest] + 1) % extent[longest]
    return result.at[tuple(place)].set(top_value)


def setup_inputs(seed: int = 0, part: int = 0) -> dict:
    key_of = jax.random.split(jax.random.key(seed), 6)
    part_keys = jax.random.split(jax.random.fold_in(key_of[5], part), 6)
    return {
        "traces": draw_traces(jax.random.fold_in(jax.random.fold_in(key_of[5], part), 71), part),
        "held_count": draw_held_count(jax.random.fold_in(jax.random.fold_in(key_of[5], part), 71), part),
        "window_owner_table": draw_window_owner_table(jax.random.fold_in(jax.random.fold_in(key_of[5], part), 71), part),
        "pick_offset": with_ends(jax.random.randint(part_keys[3], (N_EV, HCAP), 0, SEG), jax.random.fold_in(part_keys[3], 1), 0, SEG - 1).astype(jnp.int32),
        "neighbours": draw_neighbours(jax.random.fold_in(jax.random.fold_in(key_of[5], part), 71), part),
    }


def lagged(window):
    padded = jnp.pad(window, ((0, 0), (MAXLAG, MAXLAG)))
    return jnp.stack([padded[:, 2 * MAXLAG - lag_index:2 * MAXLAG - lag_index + WIN] for lag_index in range(2 * MAXLAG + 1)], axis=1)

def reference(traces, held_count, window_owner_table, pick_offset, neighbours):
    extended = jnp.pad(traces, ((0, 0), (0, WIN)))
    starts = (jnp.arange(N_EV, dtype=jnp.int32)[:, None] * SEG + pick_offset).astype(jnp.int32)

    def cut_window(offset):
        return lax.dynamic_slice(extended, (jnp.int32(0), offset.astype(jnp.int32)), (COMP, WIN))
    windows = jax.vmap(cut_window)(starts.reshape(-1))
    is_live = jnp.arange(HCAP, dtype=jnp.int32)[None, :] < held_count[:, None]
    target = jnp.where(is_live, window_owner_table, EVENTS).reshape(-1).astype(jnp.int32)
    catalog = jnp.zeros((EVENTS, COMP, WIN), jnp.bfloat16).at[target].set(windows, mode='drop')
    energy = lax.optimization_barrier(jnp.sum(jnp.square(catalog.astype(jnp.float32)), axis=2))
    inverse_norm = lax.rsqrt(energy + 1e-06)

    def correlate_event(inputs):
        event, paired_event_band = inputs
        owner_block = event // E_DEV
        paired_event = ((owner_block - paired_event_band // E_DEV) * E_DEV + paired_event_band % E_DEV).astype(jnp.int32)
        lag_shifted_traces = lagged(catalog[event].astype(jnp.float32))
        remaining_peers = catalog[paired_event].astype(jnp.float32)
        cross_products = jnp.einsum('sie,jse->sij', lag_shifted_traces, remaining_peers, precision=lax.Precision.HIGHEST)
        weight = inverse_norm[event][:, None] * inverse_norm[paired_event].T
        return lax.optimization_barrier(jnp.sum(cross_products * weight[:, None, :], axis=0))
    return lax.map(correlate_event, (jnp.arange(EVENTS, dtype=jnp.int32), neighbours))
```

```python
import functools

import jax
import jax.numpy as jnp
from jax import lax
from jax.experimental import pallas as pl
from jax.experimental.pallas import tpu as pltpu
from jax.sharding import PartitionSpec as P

WIN = 256
MAXLAG = 30
LAGS = 2 * MAXLAG + 1
SHIFTS = 16
STEPS = 4
Q_ROWS = WIN + SHIFTS * (STEPS - 1)
LANE = 128
VMEM_LIMIT = 62 * 2**20
CHUNKS = (32, 16)


ROW = 4


def from_behind(array, axis, by):
    devices = lax.axis_size(axis)
    pairs = [(i, i + by) for i in range(devices) if 0 <= i + by < devices]
    return lax.ppermute(array, axis, pairs)


def along_row(array, by):
    row = 2 * ROW
    devices = lax.axis_size("ev")
    return lax.ppermute(array, "ev", [(i, i // row * row + (i % row + 2 * by) % row) for i in range(devices)])


def between_cores(array):
    return lax.ppermute(array, "ev", [(i, i ^ 1) for i in range(lax.axis_size("ev"))])


def cut_kernel(offset_ref, owner_ref, count_ref, traces_ref, rim_ref, *refs):
    bucket_refs, ext_ref = refs[:-1], refs[-1]
    segment = traces_ref.shape[1]
    ext_ref[:, :segment] = traces_ref[...]
    ext_ref[:, segment:] = rim_ref[...]

    def cut_pair(pair, carry):
        owner = owner_ref[2 * pair]
        windows = []
        for which in range(2):
            offset = offset_ref[2 * pair + which]
            base = pl.multiple_of(offset // LANE * LANE, LANE)
            rest = offset - base
            span = ext_ref[:, pl.ds(base, WIN + LANE)].astype(jnp.float32)
            windows.append(pltpu.roll(span, WIN + LANE - rest, axis=1)[:, :WIN])
        first = 0
        for bucket_ref in bucket_refs:
            last = first + bucket_ref.shape[1] // 2
            both = jnp.concatenate([window[first:last] for window in windows], axis=0)
            bucket_ref[owner] = both.astype(jnp.bfloat16)
            first = last
        return carry

    lax.fori_loop(0, count_ref[0] // 2, cut_pair, 0)


def cut_windows(offset, owner, count, traces, rim, devices):
    components, segment = traces.shape
    return pl.pallas_call(
        cut_kernel,
        out_shape=[jax.ShapeDtypeStruct((devices, 2 * size, WIN), jnp.bfloat16) for size in CHUNKS],
        in_specs=[pl.BlockSpec(memory_space=pltpu.SMEM)] * 3 + [pl.BlockSpec(memory_space=pltpu.VMEM)] * 2,
        out_specs=[pl.BlockSpec(memory_space=pltpu.VMEM)] * len(CHUNKS),
        scratch_shapes=[pltpu.VMEM((components, segment + WIN), jnp.bfloat16)],
        compiler_params=pltpu.CompilerParams(vmem_limit_bytes=VMEM_LIMIT),
        name="cut_windows",
    )(offset, owner, count, traces, rim)


def pick_kernel(source_ref, arrived_ref, *refs):
    own_ref, rows_ref = refs[-2:]
    components, events, _ = own_ref.shape
    for event in range(events):
        source = source_ref[event]
        pair = arrived_ref[source // 2].astype(jnp.float32)
        window = jnp.where(source % 2 == 0, pair[:components], pair[components:])
        for part in range(WIN // LANE):
            rows_ref[part, pl.ds(event, components, stride=events), :] = window[:, part * LANE : (part + 1) * LANE]
    for component in range(components):
        for part in range(WIN // LANE):
            own_ref[component, :, part * LANE : (part + 1) * LANE] = rows_ref[
                part, component * events : (component + 1) * events, :
            ].astype(jnp.bfloat16)


def pick_own(source, arrived, events, after):
    components = arrived.shape[1] // 2
    return pl.pallas_call(
        pick_kernel,
        out_shape=jax.ShapeDtypeStruct((components, events, WIN), jnp.bfloat16),
        in_specs=[pl.BlockSpec(memory_space=pltpu.SMEM), pl.BlockSpec(memory_space=pltpu.VMEM)]
        + [pl.BlockSpec(memory_space=pl.ANY)] * len(after),
        out_specs=pl.BlockSpec(memory_space=pltpu.VMEM),
        scratch_shapes=[pltpu.VMEM((WIN // LANE, components * events, LANE), jnp.float32)],
        compiler_params=pltpu.CompilerParams(vmem_limit_bytes=32 * 2**20),
        name="pick_own",
    )(source, arrived, *after)


def shift_kernel(own_ref, q_ref, padded_ref, quad_ref):
    per_lane = LANE // own_ref.shape[1]
    margin = 40
    quads = quad_ref.shape[0]
    block = lax.broadcasted_iota(jnp.int32, (1, LANE), 1) // own_ref.shape[1]
    padded_ref[:margin, :] = jnp.zeros((margin, LANE), jnp.float32)
    tail = padded_ref.shape[0] - margin - WIN
    padded_ref[margin + WIN :, :] = jnp.zeros((tail, LANE), jnp.float32)
    for step in range(own_ref.shape[0]):
        window = own_ref[step].astype(jnp.float32)
        window = jnp.concatenate([window] * per_lane, axis=0)
        for part in range(WIN // LANE):
            padded_ref[margin + part * LANE : margin + (part + 1) * LANE, :] = window[
                :, part * LANE : (part + 1) * LANE
            ].T
        first = margin - 16 - 18
        quad = padded_ref[first : first + quads, :]
        for shift in range(1, per_lane):
            quad = jnp.where(block == shift, padded_ref[first - shift : first - shift + quads, :], quad)
        quad_ref[...] = quad
        for group in range(SHIFTS // per_lane):
            begin = 16 - per_lane * group
            q_ref[step, :, group * LANE : (group + 1) * LANE] = quad_ref[begin : begin + Q_ROWS, :].astype(
                jnp.bfloat16
            )


def shifted(own, batch=4):
    components, events, _ = own.shape
    width = SHIFTS * events
    return pl.pallas_call(
        shift_kernel,
        out_shape=jax.ShapeDtypeStruct((components, Q_ROWS, width), jnp.bfloat16),
        grid=(components // batch,),
        in_specs=[pl.BlockSpec((batch, events, WIN), lambda c: (c, 0, 0))],
        out_specs=pl.BlockSpec((batch, Q_ROWS, width), lambda c: (c, 0, 0)),
        scratch_shapes=[pltpu.VMEM((328, LANE), jnp.float32), pltpu.VMEM((320, LANE), jnp.float32)],
        compiler_params=pltpu.CompilerParams(vmem_limit_bytes=32 * 2**20),
        cost_estimate=pl.CostEstimate(flops=0, bytes_accessed=components * Q_ROWS * width * 4, transcendentals=0),
        name="shifted",
    )(own)


def accumulate(q_ref, pieces, band_ref, acc_ref):
    batch, events, _ = pieces[0].shape
    width = q_ref.shape[2]
    same, other = pieces[:-1], pieces[-1]
    for c in range(batch):
        for k in range(len(same)):
            band_ref[2 * k * events : (2 * k + 1) * events, :] = same[k][c]
        for k in range(other.shape[0]):
            band_ref[(2 * k + 1) * events : (2 * k + 2) * events, :] = other[k, c]
        band = band_ref[...].astype(jnp.float32)
        row_norm = lax.rsqrt(jnp.sum(band * band, axis=1, keepdims=True) + 1e-06)
        own = q_ref[c, :, :LANE].astype(jnp.float32)
        lane_norm = lax.rsqrt(jnp.sum(own * own, axis=0, keepdims=True) + 1e-06)
        weight = row_norm * lane_norm
        weight = jnp.concatenate([weight, weight], axis=1)
        for m in range(STEPS):
            begin = SHIFTS * (STEPS - 1 - m)
            for half in range(width // 256):
                products = jnp.dot(
                    band_ref[...],
                    q_ref[c, begin : begin + WIN, half * 256 : (half + 1) * 256],
                    preferred_element_type=jnp.float32,
                )
                place = m * width + half * 256
                acc_ref[:, place : place + 256] += products * weight


def partial_kernel(count, q_ref, *refs):
    pieces, (acc_ref, band_ref) = refs[:count], refs[-2:]

    @pl.when(pl.program_id(0) == 0)
    def _():
        acc_ref[...] = jnp.zeros_like(acc_ref)

    accumulate(q_ref, pieces, band_ref, acc_ref)


def final_kernel(neighbours_ref, before_ref, q_ref, *refs):
    pieces, (out_ref, band_ref, acc_ref, turned_ref) = refs[:-4], refs[-4:]
    events = pieces[0].shape[1]
    rows = band_ref.shape[0]
    step = pl.program_id(0)

    @pl.when(step == 0)
    def _():
        acc_ref[...] = before_ref[...]

    accumulate(q_ref, pieces, band_ref, acc_ref)

    @pl.when(step == pl.num_programs(0) - 1)
    def _():
        for column in range(acc_ref.shape[1] // LANE):
            for tile in range(turned_ref.shape[0]):
                first, last = tile * LANE, min((tile + 1) * LANE, rows)
                turned_ref[tile, column * LANE : (column + 1) * LANE, : last - first] = acc_ref[
                    first:last, column * LANE : (column + 1) * LANE
                ].T
        lags = STEPS * SHIFTS
        row = lax.broadcasted_iota(jnp.int32, (rows, neighbours_ref.shape[1]), 0)
        for event in range(events):
            sums = jnp.concatenate(
                [turned_ref[tile, pl.ds(event, lags, stride=events), :] for tile in range(turned_ref.shape[0])], axis=1
            )[:, :rows]
            high = sums.astype(jnp.bfloat16)
            low = (sums - high.astype(jnp.float32)).astype(jnp.bfloat16)
            chosen = (row == neighbours_ref[event : event + 1, :]).astype(jnp.bfloat16)
            both = jnp.dot(jnp.concatenate([high, low], axis=0), chosen, preferred_element_type=jnp.float32)
            total = both[:lags] + both[lags:]
            out_ref[pl.ds(event, LAGS, stride=events), :] = total[:LAGS]


def piece_specs(pieces, batch):
    same, other = pieces[:-1], pieces[-1]
    return [pl.BlockSpec((batch, *x.shape[1:]), lambda c: (c, 0, 0)) for x in same] + [
        pl.BlockSpec((other.shape[0], batch, *other.shape[2:]), lambda c: (0, c, 0, 0))
    ]


def correlate_partial(q, pieces, after, batch=4):
    components, events, _ = pieces[0].shape
    rows = (len(pieces) - 1 + pieces[-1].shape[0]) * events
    width = q.shape[2]
    return pl.pallas_call(
        functools.partial(partial_kernel, len(pieces)),
        out_shape=jax.ShapeDtypeStruct((rows, STEPS * width), jnp.float32),
        grid=(components // batch,),
        in_specs=[pl.BlockSpec((batch, Q_ROWS, width), lambda c: (c, 0, 0))]
        + piece_specs(pieces, batch)
        + [pl.BlockSpec(memory_space=pl.ANY)] * len(after),
        out_specs=pl.BlockSpec((rows, STEPS * width), lambda c: (0, 0)),
        scratch_shapes=[pltpu.VMEM((rows, WIN), jnp.bfloat16)],
        compiler_params=pltpu.CompilerParams(vmem_limit_bytes=VMEM_LIMIT),
        cost_estimate=pl.CostEstimate(
            flops=2 * components * rows * WIN * STEPS * width, bytes_accessed=12 * 2**20, transcendentals=0
        ),
        name="correlate_partial",
    )(q, *pieces, *after)


def correlate_final(neighbours, before, q, pieces, batch=4):
    components, events, _ = pieces[0].shape
    rows = (len(pieces) - 1 + pieces[-1].shape[0]) * events
    width = q.shape[2]
    k = neighbours.shape[1]
    tiles = (rows + LANE - 1) // LANE
    sums = pl.pallas_call(
        final_kernel,
        out_shape=jax.ShapeDtypeStruct((LAGS * events, k), jnp.float32),
        grid=(components // batch,),
        in_specs=[
            pl.BlockSpec((events, k), lambda c: (0, 0)),
            pl.BlockSpec((rows, STEPS * width), lambda c: (0, 0)),
            pl.BlockSpec((batch, Q_ROWS, width), lambda c: (c, 0, 0)),
        ]
        + piece_specs(pieces, batch),
        out_specs=pl.BlockSpec((LAGS * events, k), lambda c: (0, 0)),
        scratch_shapes=[
            pltpu.VMEM((rows, WIN), jnp.bfloat16),
            pltpu.VMEM((rows, STEPS * width), jnp.float32),
            pltpu.VMEM((tiles, STEPS * width, LANE), jnp.float32),
        ],
        compiler_params=pltpu.CompilerParams(vmem_limit_bytes=VMEM_LIMIT),
        cost_estimate=pl.CostEstimate(
            flops=2 * components * rows * WIN * STEPS * width, bytes_accessed=12 * 2**20, transcendentals=0
        ),
        name="correlate_final",
    )(neighbours, before, q, *pieces)
    return jnp.transpose(sums.reshape(LAGS, events, k), (1, 0, 2))


def choose_kernel(count, core_ref, *refs):
    blocks, (sent_ref, held_ref, came, went) = refs[:count], refs[-4:]
    for core in range(2):

        @pl.when(core_ref[0] == core)
        def _(core=core):
            arriving = [
                pltpu.make_async_copy(blocks[k + core], held_ref.at[k], came.at[k]) for k in range(count - 1)
            ]
            leaving = [
                pltpu.make_async_copy(held_ref.at[k], sent_ref.at[k], went.at[k]) for k in range(count - 1)
            ]
            for copy in arriving:
                copy.start()
            for k in range(count - 1):
                arriving[k].wait()
                leaving[k].start()
            for copy in leaving:
                copy.wait()


def exchange(core, blocks, after):
    sent = pl.pallas_call(
        functools.partial(choose_kernel, len(blocks)),
        out_shape=jax.ShapeDtypeStruct((len(blocks) - 1, *blocks[0].shape), blocks[0].dtype),
        in_specs=[pl.BlockSpec(memory_space=pltpu.SMEM)]
        + [pl.BlockSpec(memory_space=pl.ANY)] * (len(blocks) + len(after)),
        out_specs=pl.BlockSpec(memory_space=pl.ANY),
        scratch_shapes=[pltpu.VMEM((len(blocks) - 1, *blocks[0].shape), blocks[0].dtype)]
        + [pltpu.SemaphoreType.DMA((len(blocks) - 1,))] * 2,
        compiler_params=pltpu.CompilerParams(vmem_limit_bytes=32 * 2**20),
        name="exchange",
    )(core, *blocks, *after)
    return between_cores(sent)


def hold(array, after):
    return pl.pallas_call(
        lambda *refs: None,
        out_shape=jax.ShapeDtypeStruct(array.shape, array.dtype),
        in_specs=[pl.BlockSpec(memory_space=pl.ANY)] * (1 + len(after)),
        out_specs=pl.BlockSpec(memory_space=pl.ANY),
        input_output_aliases={0: 0},
        name="hold",
    )(array, *after)


def along_rows(y, own, above):
    sent = [jnp.where(y + by >= ROW, above, own) for by in range(1, ROW)]
    return [along_row(x, by) for by, x in enumerate(sent, 1)], sent


def spread(array):
    return lax.all_to_all(array, "ev", split_axis=0, concat_axis=0, tiled=True)


def body(traces, held_count, window_owner_table, pick_offset, neighbours):
    devices = lax.axis_size("ev")
    own_index = lax.axis_index("ev")
    held_slots = window_owner_table.shape[1]
    per_dev = neighbours.shape[0]
    next_rim = from_behind(traces[:, :WIN], "ev", -1)

    my_row = lax.dynamic_index_in_dim(window_owner_table, own_index, 0, keepdims=False)
    held_here = lax.dynamic_index_in_dim(held_count, own_index, 0, keepdims=True)
    buckets = cut_windows(pick_offset[0], my_row // per_dev, held_here, traces, next_rim, devices)

    slots = jnp.arange(held_slots, dtype=jnp.int32)
    all_live = slots[None, :] < held_count[:, None]
    wanted = own_index * per_dev + jnp.arange(per_dev, dtype=jnp.int32)
    matches = all_live[None] & (window_owner_table[None] == wanted[:, None, None])
    place = 2 * jnp.arange(devices, dtype=jnp.int32)[:, None] + slots[None, :] % 2
    source = jnp.sum(jnp.where(matches, place[None], 0), axis=(1, 2))

    y, core = own_index // 2 % ROW, (own_index % 2)[None]

    first = pick_own(source, spread(buckets[0]), per_dev, ())
    first_above = from_behind(first, "ev", 2 * ROW)
    first_q = shifted(first)
    arrived = spread(hold(buckets[1], [first_above]))
    row, _ = along_rows(y, first, first_above)
    blocks = [first, *row, first_above]
    first_pieces = blocks + [exchange(core, blocks, [first_q])]

    second = pick_own(source, arrived, per_dev, ())
    second_above = from_behind(second, "ev", 2 * ROW)
    second_q = shifted(second)
    row, sent = along_rows(y, second, second_above)
    sums = correlate_partial(first_q, first_pieces, [*sent, second_q])
    blocks = [second, *row, second_above]
    second_pieces = blocks + [exchange(core, blocks, [sums])]
    return correlate_final(neighbours, sums, second_q, second_pieces)


def solution(mesh):
    in_specs = (
        P("sta", "ev"),
        P("sta"),
        P("sta", None),
        P(("sta", "ev"), None),
        P(("sta", "ev"), None),
    )
    out_specs = P(("sta", "ev"), None, None)
    return jax.shard_map(body, mesh=mesh, in_specs=in_specs, out_specs=out_specs, check_vma=False)
```

```python
import functools

import jax
import jax.numpy as jnp
from jax import lax
from jax.experimental import pallas as pl
from jax.experimental.pallas import tpu as pltpu
from jax.sharding import PartitionSpec as P

WIN = 256
MAXLAG = 30
LAGS = 2 * MAXLAG + 1
SHIFTS = 16
STEPS = 4
Q_ROWS = WIN + SHIFTS * (STEPS - 1)
LANE = 128
VMEM_LIMIT = 24 * 2**20
LITTLE = pl.CostEstimate(flops=1, bytes_accessed=1, transcendentals=0)
TOKEN = jax.ShapeDtypeStruct((8, LANE), jnp.float32)
CHUNKS = (24, 24)


ROW = 4


def from_behind(array, axis, by):
    devices = lax.axis_size(axis)
    pairs = [(i, i + by) for i in range(devices) if 0 <= i + by < devices]
    return lax.ppermute(array, axis, pairs)


def along_row(array, by):
    row = 2 * ROW
    devices = lax.axis_size("ev")
    return lax.ppermute(array, "ev", [(i, i // row * row + (i % row + 2 * by) % row) for i in range(devices)])


def between_cores(array):
    return lax.ppermute(array, "ev", [(i, i ^ 1) for i in range(lax.axis_size("ev"))])


def cut_kernel(offset_ref, owner_ref, count_ref, traces_ref, rim_ref, bucket_ref, ext_ref):
    components, segment = traces_ref.shape
    ext_ref[:, :segment] = traces_ref[...]
    ext_ref[:, segment:] = rim_ref[...]

    def cut_pair(pair, carry):
        owner = owner_ref[2 * pair]
        for which in range(2):
            offset = offset_ref[2 * pair + which]
            base = pl.multiple_of(offset // LANE * LANE, LANE)
            rest = offset - base
            span = ext_ref[:, pl.ds(base, WIN + LANE)].astype(jnp.float32)
            span = pltpu.roll(span, WIN + LANE - rest, axis=1)
            bucket_ref[owner, which * components : (which + 1) * components, :] = span[:, :WIN].astype(
                jnp.bfloat16
            )
        return carry

    lax.fori_loop(0, count_ref[0] // 2, cut_pair, 0)


def cut_windows(offset, owner, count, traces, rim, devices):
    components, segment = traces.shape
    return pl.pallas_call(
        cut_kernel,
        out_shape=jax.ShapeDtypeStruct((devices, 2 * components, WIN), jnp.bfloat16),
        in_specs=[pl.BlockSpec(memory_space=pltpu.SMEM)] * 3 + [pl.BlockSpec(memory_space=pltpu.VMEM)] * 2,
        out_specs=pl.BlockSpec(memory_space=pltpu.VMEM),
        scratch_shapes=[pltpu.VMEM((components, segment + WIN), jnp.bfloat16)],
        cost_estimate=LITTLE,
        compiler_params=pltpu.CompilerParams(vmem_limit_bytes=60 * 2**20),
        name="cut_windows",
    )(offset, owner, count, traces, rim)


def pick_kernel(source_ref, arrived_ref, *refs):
    own_refs, rows_ref = refs[:-1], refs[-1]
    components = arrived_ref.shape[1] // 2
    events = own_refs[0].shape[1]
    for event in range(events):
        source = source_ref[event]
        half = pl.multiple_of(source % 2 * components, 16)
        window = arrived_ref[source // 2, pl.ds(half, components), :].astype(jnp.float32)
        for part in range(WIN // LANE):
            rows_ref[part, pl.ds(event, components, stride=events), :] = window[:, part * LANE : (part + 1) * LANE]
    component = 0
    for own_ref in own_refs:
        for place in range(own_ref.shape[0]):
            for part in range(WIN // LANE):
                own_ref[place, :, part * LANE : (part + 1) * LANE] = rows_ref[
                    part, component * events : (component + 1) * events, :
                ].astype(jnp.bfloat16)
            component += 1


def pick_own(source, arrived, events):
    components = arrived.shape[1] // 2
    return pl.pallas_call(
        pick_kernel,
        out_shape=[jax.ShapeDtypeStruct((size, events, WIN), jnp.bfloat16) for size in CHUNKS],
        in_specs=[pl.BlockSpec(memory_space=pltpu.SMEM), pl.BlockSpec(memory_space=pltpu.VMEM)],
        out_specs=[pl.BlockSpec(memory_space=pltpu.VMEM)] * len(CHUNKS),
        scratch_shapes=[pltpu.VMEM((WIN // LANE, components * events, LANE), jnp.float32)],
        cost_estimate=LITTLE,
        compiler_params=pltpu.CompilerParams(vmem_limit_bytes=VMEM_LIMIT),
        name="pick_own",
    )(source, arrived)


def shift_kernel(own_ref, q_ref, token_ref, padded_ref, quad_ref):
    token_ref[...] = jnp.zeros_like(token_ref)
    per_lane = LANE // own_ref.shape[1]
    margin = 40
    quads = quad_ref.shape[0]
    block = lax.broadcasted_iota(jnp.int32, (1, LANE), 1) // own_ref.shape[1]
    padded_ref[:margin, :] = jnp.zeros((margin, LANE), jnp.float32)
    tail = padded_ref.shape[0] - margin - WIN
    padded_ref[margin + WIN :, :] = jnp.zeros((tail, LANE), jnp.float32)
    for step in range(own_ref.shape[0]):
        window = own_ref[step].astype(jnp.float32)
        window = jnp.concatenate([window] * per_lane, axis=0)
        for part in range(WIN // LANE):
            padded_ref[margin + part * LANE : margin + (part + 1) * LANE, :] = window[
                :, part * LANE : (part + 1) * LANE
            ].T
        first = margin - 16 - 18
        quad = padded_ref[first : first + quads, :]
        for shift in range(1, per_lane):
            quad = jnp.where(block == shift, padded_ref[first - shift : first - shift + quads, :], quad)
        quad_ref[...] = quad
        for group in range(SHIFTS // per_lane):
            begin = 16 - per_lane * group
            q_ref[step, :, group * LANE : (group + 1) * LANE] = quad_ref[begin : begin + Q_ROWS, :].astype(
                jnp.bfloat16
            )


def shifted(own, batch=4):
    components, events, _ = own.shape
    width = SHIFTS * events
    return pl.pallas_call(
        shift_kernel,
        out_shape=[jax.ShapeDtypeStruct((components, Q_ROWS, width), jnp.bfloat16), TOKEN],
        grid=(components // batch,),
        in_specs=[pl.BlockSpec((batch, events, WIN), lambda c: (c, 0, 0))],
        out_specs=[
            pl.BlockSpec((batch, Q_ROWS, width), lambda c: (c, 0, 0)),
            pl.BlockSpec(TOKEN.shape, lambda c: (0, 0)),
        ],
        scratch_shapes=[pltpu.VMEM((328, LANE), jnp.float32), pltpu.VMEM((320, LANE), jnp.float32)],
        cost_estimate=LITTLE,
        compiler_params=pltpu.CompilerParams(vmem_limit_bytes=VMEM_LIMIT),
        name="shifted",
    )(own)


def accumulate(q_ref, pieces, band_ref, acc_ref):
    batch, events, _ = pieces[0].shape
    width = q_ref.shape[2]
    same, other = pieces[:-1], pieces[-1]
    for c in range(batch):
        for k in range(len(same)):
            band_ref[2 * k * events : (2 * k + 1) * events, :] = same[k][c]
        for k in range(other.shape[0]):
            band_ref[(2 * k + 1) * events : (2 * k + 2) * events, :] = other[k, c]
        band = band_ref[...].astype(jnp.float32)
        row_norm = lax.rsqrt(jnp.sum(band * band, axis=1, keepdims=True) + 1e-06)
        own = q_ref[c, :, :LANE].astype(jnp.float32)
        lane_norm = lax.rsqrt(jnp.sum(own * own, axis=0, keepdims=True) + 1e-06)
        weight = row_norm * lane_norm
        weight = jnp.concatenate([weight, weight], axis=1)
        for m in range(STEPS):
            begin = SHIFTS * (STEPS - 1 - m)
            for half in range(width // 256):
                products = jnp.dot(
                    band_ref[...],
                    q_ref[c, begin : begin + WIN, half * 256 : (half + 1) * 256],
                    preferred_element_type=jnp.float32,
                )
                place = m * width + half * 256
                acc_ref[:, place : place + 256] += products * weight


def partial_kernel(started, count, q_ref, *refs):
    acc_ref, token_ref, band_ref = refs[-3:]

    @pl.when(pl.program_id(0) == 0)
    def _():
        token_ref[...] = jnp.zeros_like(token_ref)
        acc_ref[...] = refs[0][...] if started else jnp.zeros_like(acc_ref)

    accumulate(q_ref, refs[started : started + count], band_ref, acc_ref)


def final_kernel(neighbours_ref, before_ref, q_ref, *refs):
    pieces, (out_ref, band_ref, acc_ref, turned_ref, spread_ref) = refs[:-5], refs[-5:]
    events = pieces[0].shape[1]
    rows = band_ref.shape[0]
    step = pl.program_id(0)

    @pl.when(step == 0)
    def _():
        acc_ref[...] = before_ref[...]

    accumulate(q_ref, pieces, band_ref, acc_ref)

    @pl.when(step == pl.num_programs(0) - 1)
    def _():
        for column in range(acc_ref.shape[1] // LANE):
            for tile in range(turned_ref.shape[0]):
                first, last = tile * LANE, min((tile + 1) * LANE, rows)
                turned_ref[tile, column * LANE : (column + 1) * LANE, : last - first] = acc_ref[
                    first:last, column * LANE : (column + 1) * LANE
                ].T
        lags = STEPS * SHIFTS
        row = lax.broadcasted_iota(jnp.int32, (rows, neighbours_ref.shape[1]), 0)
        for event in range(events):
            sums = jnp.concatenate(
                [turned_ref[tile, pl.ds(event, lags, stride=events), :] for tile in range(turned_ref.shape[0])], axis=1
            )[:, :rows]
            high = sums.astype(jnp.bfloat16)
            low = (sums - high.astype(jnp.float32)).astype(jnp.bfloat16)
            chosen = (row == neighbours_ref[event : event + 1, :]).astype(jnp.bfloat16)
            both = jnp.dot(jnp.concatenate([high, low], axis=0), chosen, preferred_element_type=jnp.float32)
            total = both[:lags] + both[lags:]
            spread_ref[pl.ds(event, lags, stride=events), :] = total
        out_ref[...] = spread_ref[: LAGS * events]


def piece_specs(pieces, batch):
    same, other = pieces[:-1], pieces[-1]
    return [pl.BlockSpec((batch, *x.shape[1:]), lambda c: (c, 0, 0)) for x in same] + [
        pl.BlockSpec((other.shape[0], batch, *other.shape[2:]), lambda c: (0, c, 0, 0))
    ]


def correlate_partial(before, q, pieces, after, batch=4):
    components, events, _ = pieces[0].shape
    rows = (len(pieces) - 1 + pieces[-1].shape[0]) * events
    width = q.shape[2]
    sums = pl.BlockSpec((rows, STEPS * width), lambda c: (0, 0))
    return pl.pallas_call(
        functools.partial(partial_kernel, len(before), len(pieces)),
        out_shape=[jax.ShapeDtypeStruct((rows, STEPS * width), jnp.float32), TOKEN],
        grid=(components // batch,),
        in_specs=[pl.BlockSpec((batch, Q_ROWS, width), lambda c: (c, 0, 0))]
        + [sums] * len(before)
        + piece_specs(pieces, batch)
        + [pl.BlockSpec(memory_space=pl.ANY)] * len(after),
        out_specs=[sums, pl.BlockSpec(TOKEN.shape, lambda c: (0, 0))],
        scratch_shapes=[pltpu.VMEM((rows, WIN), jnp.bfloat16)],
        cost_estimate=LITTLE,
        compiler_params=pltpu.CompilerParams(vmem_limit_bytes=VMEM_LIMIT),
        name="correlate_partial",
    )(q, *before, *pieces, *after)


def correlate_final(neighbours, before, q, pieces, batch=4):
    components, events, _ = pieces[0].shape
    rows = (len(pieces) - 1 + pieces[-1].shape[0]) * events
    width = q.shape[2]
    k = neighbours.shape[1]
    tiles = (rows + LANE - 1) // LANE
    sums = pl.pallas_call(
        final_kernel,
        out_shape=jax.ShapeDtypeStruct((LAGS * events, k), jnp.float32),
        grid=(components // batch,),
        in_specs=[
            pl.BlockSpec((events, k), lambda c: (0, 0)),
            pl.BlockSpec((rows, STEPS * width), lambda c: (0, 0)),
            pl.BlockSpec((batch, Q_ROWS, width), lambda c: (c, 0, 0)),
        ]
        + piece_specs(pieces, batch),
        out_specs=pl.BlockSpec((LAGS * events, k), lambda c: (0, 0)),
        scratch_shapes=[
            pltpu.VMEM((rows, WIN), jnp.bfloat16),
            pltpu.VMEM((rows, STEPS * width), jnp.float32),
            pltpu.VMEM((tiles, STEPS * width, LANE), jnp.float32),
            pltpu.VMEM((STEPS * width, k), jnp.float32),
        ],
        cost_estimate=LITTLE,
        compiler_params=pltpu.CompilerParams(vmem_limit_bytes=VMEM_LIMIT),
        name="correlate_final",
    )(neighbours, before, q, *pieces)
    return jnp.transpose(sums.reshape(LAGS, events, k), (1, 0, 2))


def exchange_kernel(count, core_ref, *refs):
    blocks, sent_ref = refs[:count], refs[-1]
    for core in range(2):

        @pl.when(core_ref[0] == core)
        def _(core=core):
            for k in range(count - 1):
                sent_ref[k] = blocks[k + core][...]


def exchange(core, blocks, after):
    sent = pl.pallas_call(
        functools.partial(exchange_kernel, len(blocks)),
        out_shape=jax.ShapeDtypeStruct((len(blocks) - 1, *blocks[0].shape), blocks[0].dtype),
        in_specs=[pl.BlockSpec(memory_space=pltpu.SMEM)]
        + [pl.BlockSpec(memory_space=pltpu.VMEM)] * len(blocks)
        + [pl.BlockSpec(memory_space=pl.ANY)] * len(after),
        out_specs=pl.BlockSpec(memory_space=pltpu.VMEM),
        cost_estimate=LITTLE,
        compiler_params=pltpu.CompilerParams(vmem_limit_bytes=VMEM_LIMIT),
        name="exchange",
    )(core, *blocks, *after)
    return between_cores(sent)


def row_kernel(y_ref, own_ref, above_ref, *refs):
    sent, token_ref = refs[-ROW:-1], refs[-1]
    for by in range(1, ROW):

        @pl.when(y_ref[0] + by >= ROW)
        def _(by=by):
            sent[by - 1][...] = above_ref[...]

        @pl.when(y_ref[0] + by < ROW)
        def _(by=by):
            sent[by - 1][...] = own_ref[...]

    token_ref[...] = jnp.zeros_like(token_ref)


def along_rows(y, own, above, after):
    *sent, token = pl.pallas_call(
        row_kernel,
        out_shape=[jax.ShapeDtypeStruct(own.shape, own.dtype)] * (ROW - 1) + [TOKEN],
        in_specs=[pl.BlockSpec(memory_space=pltpu.SMEM)]
        + [pl.BlockSpec(memory_space=pltpu.VMEM)] * 2
        + [pl.BlockSpec(memory_space=pl.ANY)] * len(after),
        out_specs=[pl.BlockSpec(memory_space=pltpu.VMEM)] * ROW,
        cost_estimate=LITTLE,
        compiler_params=pltpu.CompilerParams(vmem_limit_bytes=VMEM_LIMIT),
        name="along_rows",
    )(y, own, above, *after)
    return [along_row(x, by) for by, x in enumerate(sent, 1)], token


def body(traces, held_count, window_owner_table, pick_offset, neighbours):
    devices = lax.axis_size("ev")
    own_index = lax.axis_index("ev")
    held_slots = window_owner_table.shape[1]
    per_dev = neighbours.shape[0]
    next_rim = from_behind(traces[:, :WIN], "ev", -1)

    my_row = lax.dynamic_index_in_dim(window_owner_table, own_index, 0, keepdims=False)
    held_here = lax.dynamic_index_in_dim(held_count, own_index, 0, keepdims=True)
    bucket = cut_windows(pick_offset[0], my_row // per_dev, held_here, traces, next_rim, devices)
    arrived = lax.all_to_all(bucket, "ev", split_axis=0, concat_axis=0, tiled=True)

    slots = jnp.arange(held_slots, dtype=jnp.int32)
    all_live = slots[None, :] < held_count[:, None]
    wanted = own_index * per_dev + jnp.arange(per_dev, dtype=jnp.int32)
    matches = all_live[None] & (window_owner_table[None] == wanted[:, None, None])
    place = 2 * jnp.arange(devices, dtype=jnp.int32)[:, None] + slots[None, :] % 2
    source = jnp.sum(jnp.where(matches, place[None], 0), axis=(1, 2))

    y, core = (own_index // 2 % ROW)[None], (own_index % 2)[None]

    owns = pick_own(source, arrived, per_dev)
    aboves = [from_behind(own, "ev", 2 * ROW) for own in owns]
    shifts = [shifted(own) for own in owns]
    rows, sent = [], []
    for index, (own, above) in enumerate(zip(owns, aboves)):
        row, token = along_rows(y, own, above, [shifts[index][1]])
        rows.append(row)
        sent.append(token)
    last = len(owns) - 1
    sums, summed = [], []
    for index in range(last + 1):
        blocks = [owns[index], *rows[index], aboves[index]]
        pieces = blocks + [exchange(core, blocks, summed + [sent[min(index + 1, last)]])]
        if index == last:
            return correlate_final(neighbours, *sums, shifts[index][0], pieces)
        total, token = correlate_partial(sums, shifts[index][0], pieces, [sent[min(index + 2, last)]])
        sums, summed = [total], [token]


def solution(mesh):
    in_specs = (
        P("sta", "ev"),
        P("sta"),
        P("sta", None),
        P(("sta", "ev"), None),
        P(("sta", "ev"), None),
    )
    out_specs = P(("sta", "ev"), None, None)
    return jax.shard_map(body, mesh=mesh, in_specs=in_specs, out_specs=out_specs, check_vma=False)
```

```python
import functools

import jax
import jax.numpy as jnp
from jax import lax
from jax.experimental import pallas as pl
from jax.experimental.pallas import tpu as pltpu
from jax.sharding import PartitionSpec as P

WIN = 256
MAXLAG = 30
LAGS = 2 * MAXLAG + 1
SHIFTS = 16
STEPS = 4
Q_ROWS = WIN + SHIFTS * (STEPS - 1)
LANE = 128
VMEM_LIMIT = 24 * 2**20
LITTLE = pl.CostEstimate(flops=1, bytes_accessed=1, transcendentals=0)
TOKEN = jax.ShapeDtypeStruct((8, LANE), jnp.float32)
CHUNKS = (24, 24)


ROW = 4


def from_behind(array, axis, by):
    devices = lax.axis_size(axis)
    pairs = [(i, i + by) for i in range(devices) if 0 <= i + by < devices]
    return lax.ppermute(array, axis, pairs)


def along_row(array, by):
    row = 2 * ROW
    devices = lax.axis_size("ev")
    return lax.ppermute(array, "ev", [(i, i // row * row + (i % row + 2 * by) % row) for i in range(devices)])


def between_cores(array):
    return lax.ppermute(array, "ev", [(i, i ^ 1) for i in range(lax.axis_size("ev"))])


def cut_kernel(offset_ref, owner_ref, count_ref, traces_ref, rim_ref, bucket_ref, ext_ref):
    components, segment = traces_ref.shape
    ext_ref[:, :segment] = traces_ref[...]
    ext_ref[:, segment:] = rim_ref[...]

    def cut_pair(pair, carry):
        owner = owner_ref[2 * pair]
        for which in range(2):
            offset = offset_ref[2 * pair + which]
            base = pl.multiple_of(offset // LANE * LANE, LANE)
            rest = offset - base
            span = ext_ref[:, pl.ds(base, WIN + LANE)].astype(jnp.float32)
            span = pltpu.roll(span, WIN + LANE - rest, axis=1)
            bucket_ref[owner, which * components : (which + 1) * components, :] = span[:, :WIN].astype(
                jnp.bfloat16
            )
        return carry

    lax.fori_loop(0, count_ref[0] // 2, cut_pair, 0)


def cut_windows(offset, owner, count, traces, rim, devices):
    components, segment = traces.shape
    return pl.pallas_call(
        cut_kernel,
        out_shape=jax.ShapeDtypeStruct((devices, 2 * components, WIN), jnp.bfloat16),
        in_specs=[pl.BlockSpec(memory_space=pltpu.SMEM)] * 3 + [pl.BlockSpec(memory_space=pltpu.VMEM)] * 2,
        out_specs=pl.BlockSpec(memory_space=pltpu.VMEM),
        scratch_shapes=[pltpu.VMEM((components, segment + WIN), jnp.bfloat16)],
        cost_estimate=LITTLE,
        compiler_params=pltpu.CompilerParams(vmem_limit_bytes=60 * 2**20),
        name="cut_windows",
    )(offset, owner, count, traces, rim)


def pick_kernel(source_ref, arrived_ref, *refs):
    own_refs, rows_ref = refs[:-1], refs[-1]
    components = arrived_ref.shape[1] // 2
    events = own_refs[0].shape[1]
    for event in range(events):
        source = source_ref[event]
        half = pl.multiple_of(source % 2 * components, 16)
        window = arrived_ref[source // 2, pl.ds(half, components), :].astype(jnp.float32)
        for part in range(WIN // LANE):
            rows_ref[part, pl.ds(event, components, stride=events), :] = window[:, part * LANE : (part + 1) * LANE]
    component = 0
    for own_ref in own_refs:
        for place in range(own_ref.shape[0]):
            for part in range(WIN // LANE):
                own_ref[place, :, part * LANE : (part + 1) * LANE] = rows_ref[
                    part, component * events : (component + 1) * events, :
                ].astype(jnp.bfloat16)
            component += 1


def pick_own(source, arrived, events):
    components = arrived.shape[1] // 2
    return pl.pallas_call(
        pick_kernel,
        out_shape=[jax.ShapeDtypeStruct((size, events, WIN), jnp.bfloat16) for size in CHUNKS],
        in_specs=[pl.BlockSpec(memory_space=pltpu.SMEM), pl.BlockSpec(memory_space=pltpu.VMEM)],
        out_specs=[pl.BlockSpec(memory_space=pltpu.VMEM)] * len(CHUNKS),
        scratch_shapes=[pltpu.VMEM((WIN // LANE, components * events, LANE), jnp.float32)],
        cost_estimate=LITTLE,
        compiler_params=pltpu.CompilerParams(vmem_limit_bytes=VMEM_LIMIT),
        name="pick_own",
    )(source, arrived)


def shift_kernel(own_ref, q_ref, token_ref, padded_ref, quad_ref):
    token_ref[...] = jnp.zeros_like(token_ref)
    per_lane = LANE // own_ref.shape[1]
    margin = 40
    quads = quad_ref.shape[0]
    block = lax.broadcasted_iota(jnp.int32, (1, LANE), 1) // own_ref.shape[1]
    padded_ref[:margin, :] = jnp.zeros((margin, LANE), jnp.float32)
    tail = padded_ref.shape[0] - margin - WIN
    padded_ref[margin + WIN :, :] = jnp.zeros((tail, LANE), jnp.float32)
    for step in range(own_ref.shape[0]):
        window = own_ref[step].astype(jnp.float32)
        window = jnp.concatenate([window] * per_lane, axis=0)
        for part in range(WIN // LANE):
            padded_ref[margin + part * LANE : margin + (part + 1) * LANE, :] = window[
                :, part * LANE : (part + 1) * LANE
            ].T
        first = margin - 16 - 18
        quad = padded_ref[first : first + quads, :]
        for shift in range(1, per_lane):
            quad = jnp.where(block == shift, padded_ref[first - shift : first - shift + quads, :], quad)
        quad_ref[...] = quad
        for group in range(SHIFTS // per_lane):
            begin = 16 - per_lane * group
            q_ref[step, :, group * LANE : (group + 1) * LANE] = quad_ref[begin : begin + Q_ROWS, :].astype(
                jnp.bfloat16
            )


def shifted(own, batch=4):
    components, events, _ = own.shape
    width = SHIFTS * events
    return pl.pallas_call(
        shift_kernel,
        out_shape=[jax.ShapeDtypeStruct((components, Q_ROWS, width), jnp.bfloat16), TOKEN],
        grid=(components // batch,),
        in_specs=[pl.BlockSpec((batch, events, WIN), lambda c: (c, 0, 0))],
        out_specs=[
            pl.BlockSpec((batch, Q_ROWS, width), lambda c: (c, 0, 0)),
            pl.BlockSpec(TOKEN.shape, lambda c: (0, 0)),
        ],
        scratch_shapes=[pltpu.VMEM((328, LANE), jnp.float32), pltpu.VMEM((320, LANE), jnp.float32)],
        cost_estimate=LITTLE,
        compiler_params=pltpu.CompilerParams(vmem_limit_bytes=VMEM_LIMIT),
        name="shifted",
    )(own)


def accumulate(q_ref, pieces, band_ref, acc_ref):
    batch, events, _ = pieces[0].shape
    width = q_ref.shape[2]
    same, other = pieces[:-1], pieces[-1]
    for c in range(batch):
        for k in range(len(same)):
            band_ref[2 * k * events : (2 * k + 1) * events, :] = same[k][c]
        for k in range(other.shape[0]):
            band_ref[(2 * k + 1) * events : (2 * k + 2) * events, :] = other[k, c]
        band = band_ref[...].astype(jnp.float32)
        row_norm = lax.rsqrt(jnp.sum(band * band, axis=1, keepdims=True) + 1e-06)
        own = q_ref[c, :, :LANE].astype(jnp.float32)
        lane_norm = lax.rsqrt(jnp.sum(own * own, axis=0, keepdims=True) + 1e-06)
        weight = row_norm * lane_norm
        weight = jnp.concatenate([weight, weight], axis=1)
        for m in range(STEPS):
            begin = SHIFTS * (STEPS - 1 - m)
            for half in range(width // 256):
                products = jnp.dot(
                    band_ref[...],
                    q_ref[c, begin : begin + WIN, half * 256 : (half + 1) * 256],
                    preferred_element_type=jnp.float32,
                )
                place = m * width + half * 256
                acc_ref[:, place : place + 256] += products * weight


def partial_kernel(started, count, q_ref, *refs):
    acc_ref, token_ref, band_ref = refs[-3:]

    @pl.when(pl.program_id(0) == 0)
    def _():
        token_ref[...] = jnp.zeros_like(token_ref)
        acc_ref[...] = refs[0][...] if started else jnp.zeros_like(acc_ref)

    accumulate(q_ref, refs[started : started + count], band_ref, acc_ref)


def final_kernel(neighbours_ref, before_ref, q_ref, *refs):
    pieces, (out_ref, band_ref, acc_ref, turned_ref, spread_ref) = refs[:-5], refs[-5:]
    events = pieces[0].shape[1]
    rows = band_ref.shape[0]
    step = pl.program_id(0)

    @pl.when(step == 0)
    def _():
        acc_ref[...] = before_ref[...]

    accumulate(q_ref, pieces, band_ref, acc_ref)

    @pl.when(step == pl.num_programs(0) - 1)
    def _():
        for column in range(acc_ref.shape[1] // LANE):
            for tile in range(turned_ref.shape[0]):
                first, last = tile * LANE, min((tile + 1) * LANE, rows)
                turned_ref[tile, column * LANE : (column + 1) * LANE, : last - first] = acc_ref[
                    first:last, column * LANE : (column + 1) * LANE
                ].T
        lags = STEPS * SHIFTS
        row = lax.broadcasted_iota(jnp.int32, (rows, neighbours_ref.shape[1]), 0)
        for event in range(events):
            sums = jnp.concatenate(
                [turned_ref[tile, pl.ds(event, lags, stride=events), :] for tile in range(turned_ref.shape[0])], axis=1
            )[:, :rows]
            high = sums.astype(jnp.bfloat16)
            low = (sums - high.astype(jnp.float32)).astype(jnp.bfloat16)
            chosen = (row == neighbours_ref[event : event + 1, :]).astype(jnp.bfloat16)
            both = jnp.dot(jnp.concatenate([high, low], axis=0), chosen, preferred_element_type=jnp.float32)
            total = both[:lags] + both[lags:]
            spread_ref[pl.ds(event, lags, stride=events), :] = total
        out_ref[...] = spread_ref[: LAGS * events]


def piece_specs(pieces, batch):
    same, other = pieces[:-1], pieces[-1]
    return [pl.BlockSpec((batch, *x.shape[1:]), lambda c: (c, 0, 0)) for x in same] + [
        pl.BlockSpec((other.shape[0], batch, *other.shape[2:]), lambda c: (0, c, 0, 0))
    ]


def correlate_partial(before, q, pieces, after, batch=4):
    components, events, _ = pieces[0].shape
    rows = (len(pieces) - 1 + pieces[-1].shape[0]) * events
    width = q.shape[2]
    sums = pl.BlockSpec((rows, STEPS * width), lambda c: (0, 0))
    return pl.pallas_call(
        functools.partial(partial_kernel, len(before), len(pieces)),
        out_shape=[jax.ShapeDtypeStruct((rows, STEPS * width), jnp.float32), TOKEN],
        grid=(components // batch,),
        in_specs=[pl.BlockSpec((batch, Q_ROWS, width), lambda c: (c, 0, 0))]
        + [sums] * len(before)
        + piece_specs(pieces, batch)
        + [pl.BlockSpec(memory_space=pl.ANY)] * len(after),
        out_specs=[sums, pl.BlockSpec(TOKEN.shape, lambda c: (0, 0))],
        scratch_shapes=[pltpu.VMEM((rows, WIN), jnp.bfloat16)],
        cost_estimate=pl.CostEstimate(
            flops=2 * components * rows * WIN * STEPS * width, bytes_accessed=12 * 2**20, transcendentals=0
        ),
        compiler_params=pltpu.CompilerParams(vmem_limit_bytes=VMEM_LIMIT),
        name="correlate_partial",
    )(q, *before, *pieces, *after)


def correlate_final(neighbours, before, q, pieces, batch=4):
    components, events, _ = pieces[0].shape
    rows = (len(pieces) - 1 + pieces[-1].shape[0]) * events
    width = q.shape[2]
    k = neighbours.shape[1]
    tiles = (rows + LANE - 1) // LANE
    sums = pl.pallas_call(
        final_kernel,
        out_shape=jax.ShapeDtypeStruct((LAGS * events, k), jnp.float32),
        grid=(components // batch,),
        in_specs=[
            pl.BlockSpec((events, k), lambda c: (0, 0)),
            pl.BlockSpec((rows, STEPS * width), lambda c: (0, 0)),
            pl.BlockSpec((batch, Q_ROWS, width), lambda c: (c, 0, 0)),
        ]
        + piece_specs(pieces, batch),
        out_specs=pl.BlockSpec((LAGS * events, k), lambda c: (0, 0)),
        scratch_shapes=[
            pltpu.VMEM((rows, WIN), jnp.bfloat16),
            pltpu.VMEM((rows, STEPS * width), jnp.float32),
            pltpu.VMEM((tiles, STEPS * width, LANE), jnp.float32),
            pltpu.VMEM((STEPS * width, k), jnp.float32),
        ],
        cost_estimate=pl.CostEstimate(
            flops=2 * components * rows * WIN * STEPS * width, bytes_accessed=12 * 2**20, transcendentals=0
        ),
        compiler_params=pltpu.CompilerParams(vmem_limit_bytes=VMEM_LIMIT),
        name="correlate_final",
    )(neighbours, before, q, *pieces)
    return jnp.transpose(sums.reshape(LAGS, events, k), (1, 0, 2))


def exchange_kernel(count, core_ref, *refs):
    blocks, sent_ref = refs[:count], refs[-1]
    for core in range(2):

        @pl.when(core_ref[0] == core)
        def _(core=core):
            for k in range(count - 1):
                sent_ref[k] = blocks[k + core][...]


def exchange(core, blocks, after):
    sent = pl.pallas_call(
        functools.partial(exchange_kernel, len(blocks)),
        out_shape=jax.ShapeDtypeStruct((len(blocks) - 1, *blocks[0].shape), blocks[0].dtype),
        in_specs=[pl.BlockSpec(memory_space=pltpu.SMEM)]
        + [pl.BlockSpec(memory_space=pltpu.VMEM)] * len(blocks)
        + [pl.BlockSpec(memory_space=pl.ANY)] * len(after),
        out_specs=pl.BlockSpec(memory_space=pltpu.VMEM),
        cost_estimate=LITTLE,
        compiler_params=pltpu.CompilerParams(vmem_limit_bytes=VMEM_LIMIT),
        name="exchange",
    )(core, *blocks, *after)
    return between_cores(sent)


def row_kernel(y_ref, own_ref, above_ref, *refs):
    sent, token_ref = refs[-ROW:-1], refs[-1]
    for by in range(1, ROW):

        @pl.when(y_ref[0] + by >= ROW)
        def _(by=by):
            sent[by - 1][...] = above_ref[...]

        @pl.when(y_ref[0] + by < ROW)
        def _(by=by):
            sent[by - 1][...] = own_ref[...]

    token_ref[...] = jnp.zeros_like(token_ref)


def along_rows(y, own, above, after):
    *sent, token = pl.pallas_call(
        row_kernel,
        out_shape=[jax.ShapeDtypeStruct(own.shape, own.dtype)] * (ROW - 1) + [TOKEN],
        in_specs=[pl.BlockSpec(memory_space=pltpu.SMEM)]
        + [pl.BlockSpec(memory_space=pltpu.VMEM)] * 2
        + [pl.BlockSpec(memory_space=pl.ANY)] * len(after),
        out_specs=[pl.BlockSpec(memory_space=pltpu.VMEM)] * ROW,
        cost_estimate=LITTLE,
        compiler_params=pltpu.CompilerParams(vmem_limit_bytes=VMEM_LIMIT),
        name="along_rows",
    )(y, own, above, *after)
    return [along_row(x, by) for by, x in enumerate(sent, 1)], token


def body(traces, held_count, window_owner_table, pick_offset, neighbours):
    devices = lax.axis_size("ev")
    own_index = lax.axis_index("ev")
    held_slots = window_owner_table.shape[1]
    per_dev = neighbours.shape[0]
    next_rim = from_behind(traces[:, :WIN], "ev", -1)

    my_row = lax.dynamic_index_in_dim(window_owner_table, own_index, 0, keepdims=False)
    held_here = lax.dynamic_index_in_dim(held_count, own_index, 0, keepdims=True)
    bucket = cut_windows(pick_offset[0], my_row // per_dev, held_here, traces, next_rim, devices)
    arrived = lax.all_to_all(bucket, "ev", split_axis=0, concat_axis=0, tiled=True)

    slots = jnp.arange(held_slots, dtype=jnp.int32)
    all_live = slots[None, :] < held_count[:, None]
    wanted = own_index * per_dev + jnp.arange(per_dev, dtype=jnp.int32)
    matches = all_live[None] & (window_owner_table[None] == wanted[:, None, None])
    place = 2 * jnp.arange(devices, dtype=jnp.int32)[:, None] + slots[None, :] % 2
    source = jnp.sum(jnp.where(matches, place[None], 0), axis=(1, 2))

    y, core = (own_index // 2 % ROW)[None], (own_index % 2)[None]

    owns = pick_own(source, arrived, per_dev)
    aboves = [from_behind(own, "ev", 2 * ROW) for own in owns]
    shifts = [shifted(own) for own in owns]
    rows, sent = [], []
    for index, (own, above) in enumerate(zip(owns, aboves)):
        row, token = along_rows(y, own, above, [shifts[index][1]])
        rows.append(row)
        sent.append(token)
    last = len(owns) - 1
    sums, summed = [], []
    for index in range(last + 1):
        blocks = [owns[index], *rows[index], aboves[index]]
        pieces = blocks + [exchange(core, blocks, summed + [sent[min(index + 1, last)]])]
        if index == last:
            return correlate_final(neighbours, *sums, shifts[index][0], pieces)
        total, token = correlate_partial(sums, shifts[index][0], pieces, [sent[min(index + 2, last)]])
        sums, summed = [total], [token]


def solution(mesh):
    in_specs = (
        P("sta", "ev"),
        P("sta"),
        P("sta", None),
        P(("sta", "ev"), None),
        P(("sta", "ev"), None),
    )
    out_specs = P(("sta", "ev"), None, None)
    return jax.shard_map(body, mesh=mesh, in_specs=in_specs, out_specs=out_specs, check_vma=False)
```
